128 devices in a mesh: rep: 2 (over x_lo), row: 64 (over z, y, x_hi, core).
Axes of the slice: x: 4 (x_hi: 2, x_lo: 2; x = x_hi * 2 + x_lo), y: 4, z: 4, core: 2. Of those that a mesh axis runs over, the one named last changes fastest.
Arguments:
- features: bfloat16 [131072, 128], P(('row', 'rep')), may hold values from -6 to 6
- blocks: bfloat16 [64, 2, 64, 2, 256, 256], P('row', 'rep'), may hold values from 0 to 0.049804688
- codes: int32 [64, 2, 64, 2], P('row', 'rep'), may hold values from 0 to 31, as said below
- counts: int32 [64, 2, 64], P('row', 'rep'), may hold values from 0 to 2
- weight: bfloat16 [128, 256], replicated, may hold values from -0.5 to 0.5
- bias: float32 [256], replicated, may hold values from -3 to 3
Outputs:
- mixed: bfloat16 [131072, 256], P(('row', 'rep'))
The draws below stay inside these ranges and needn't reach their ends.
Inputs may be any that keep to these rules, and one draw needn't show every extreme that they name: `codes`: each slot names row block and column block as rowblock * 4 + colblock; the slots of one device and section are distinct; slots at or past the section's count are unused.
All inputs are finite; a program needn't handle non-finite values.
Results may differ from the reference program's by a relative error of at most 0.014.
Values may be sent and summed in bfloat16 or wider, within the bound.
No kernel may reach another device: no remote copies, remote signals or barrier semaphores. Data moves between devices by JAX's collectives and lax.ppermute only.
A program may use at most 128 MiB of HBM per device.

```python
import jax
import jax.numpy as jnp
from jax import lax

F = 128
H = 256
BLOCK = 256
SLOTS = 2
ROWS_DEV = 1024
NODES = 131072
PAIRS = 32
N_REP = 2
N_ROW = 64


def draw_counts(key, part):
    key = jax.random.fold_in(key, 11)
    subkeys = jax.random.split(key, 3)
    levels = jax.random.randint(subkeys[0], (N_ROW, N_REP, 1, 1), 0, 4)
    heavy = jnp.left_shift(jnp.ones_like(levels), levels)
    chosen_row = jax.random.randint(subkeys[1], (), 0, N_ROW)
    heavy = jnp.where(jnp.arange(N_ROW)[:, None, None, None] == chosen_row, 8, heavy)
    trials = jax.random.randint(subkeys[2], (N_ROW, N_REP, N_ROW, SLOTS), 0, 8)
    return jnp.sum((trials < heavy).astype(jnp.int32), axis=-1).astype(jnp.int32)


def draw_codes(key, part):
    key = jax.random.fold_in(key, 23)
    scores = jax.random.randint(key, (N_ROW, N_REP, N_ROW, PAIRS), 0, 1048576) * PAIRS + jnp.arange(PAIRS, dtype=jnp.int32)
    ranking = jnp.argsort(scores, axis=-1, stable=True)[..., :SLOTS].astype(jnp.int32)
    forced = ((PAIRS - 1 + jnp.arange(SLOTS, dtype=jnp.int32)) % PAIRS).astype(jnp.int32)
    return ranking.at[0, 0, 0].set(forced)


def steps_of(stream_key, extent, cuts, smallest, top_value):
    loudness = 1.0
    for position, blocks in cuts:
        steps = jax.random.uniform(jax.random.fold_in(jax.random.fold_in(stream_key, 6), position), (blocks,), jnp.float32, smallest / len(cuts), top_value / len(cuts))
        loudness = loudness * jnp.repeat(jnp.exp(steps), extent[position] // blocks).reshape((-1,) + (1,) * (len(extent) - 1 - position))
    return loudness


def centred(own_key, dims, scale, limit, shards=(), kind=jnp.bfloat16):
    drawn = jax.random.normal(own_key, dims, jnp.float32) * scale
    if len(shards) > 0:
        drawn = steps_of(own_key, dims, shards, -0.22, 0.18) * drawn
    return jnp.clip(drawn, min=-limit, max=limit).astype(kind)


def setup_inputs(seed: int = 0) -> dict:
    key_list = jax.random.split(jax.random.key(seed), 7)
    return {
        "features": centred(key_list[0], (NODES, F), 1.0, 6.0, ((0, 128),)),
        "blocks": jnp.clip(0.049804688 * jax.random.uniform(key_list[1], (N_ROW, N_REP, N_ROW, SLOTS, BLOCK, BLOCK), jnp.float32) ** steps_of(key_list[1], (N_ROW, N_REP, N_ROW, SLOTS, BLOCK, BLOCK), ((0, 64), (1, 2)), -0.2, 0.2), 0.0, 0.049804688).astype(jnp.bfloat16),
        "codes": draw_codes(jax.random.fold_in(key_list[6], 71), 0),
        "counts": draw_counts(jax.random.fold_in(key_list[6], 71), 0),
        "weight": centred(key_list[4], (F, H), F ** -0.5, 0.5),
        "bias": centred(key_list[5], (H,), 0.5, 3.0, (), jnp.float32),
    }


def aggregate(tiles, weights, chosen, living, col_blocks, row_blocks):
    columns = chosen % col_blocks
    targets = chosen // col_blocks
    selector = (columns[..., None] == jnp.arange(col_blocks, dtype=jnp.int32)).astype(jnp.float32)
    picked = jnp.einsum("skc,scbf->skbf", selector, tiles)
    product = jnp.einsum("skuv,skvf->skuf", weights.astype(jnp.float32), picked)
    active = (jnp.arange(weights.shape[1], dtype=jnp.int32)[None, :] < living[:, None]).astype(jnp.float32)
    placing = (targets[..., None] == jnp.arange(row_blocks, dtype=jnp.int32)).astype(jnp.float32) * active[..., None]
    return jnp.einsum("skr,skuf->ruf", placing, product)


def reference(features, blocks, codes, counts, weight, bias):
    col_blocks = ROWS_DEV // BLOCK
    row_blocks = N_REP * ROWS_DEV // BLOCK
    tiles = features.astype(jnp.float32).reshape(N_ROW, N_REP, col_blocks, BLOCK, F)

    def one_row(bundle):
        weights, chosen, living = bundle
        summed = jnp.zeros((row_blocks, BLOCK, F), jnp.float32)
        for rep_index in range(N_REP):
            summed = summed + aggregate(tiles[:, rep_index], weights[rep_index], chosen[rep_index], living[rep_index], col_blocks, row_blocks)
        return summed

    sums = lax.map(one_row, (blocks, codes, counts))
    gathered = sums.reshape(N_ROW * N_REP * ROWS_DEV, F).astype(jnp.bfloat16)
    hidden = jnp.dot(gathered, weight, preferred_element_type=jnp.float32) + bias
    return jnp.maximum(hidden, 0.0).astype(jnp.bfloat16)
```

```python
import functools

import jax
import jax.numpy as jnp
import numpy as np
from jax import lax
from jax.experimental import pallas as pl
from jax.experimental.pallas import tpu as pltpu
from jax.sharding import PartitionSpec as P

DIMS = (4, 4, 2, 2)
SLOTS = 2

HOME = (0, 0, 0)
ROUNDS = (
    (("P1", (HOME,)), ("M1", (HOME,)), ("X", (HOME,)), ("P2", (HOME,)), ("M2", (HOME,))),
    (
        ("P1", ((0, 0, 3), (0, 0, 1))),
        ("M1", ((0, 1, 0), (0, 0, 1))),
        ("X", ((0, 0, 3), (0, 0, 1))),
        ("P2", ((1, 0, 0), (0, 1, 0))),
        ("M2", ((1, 0, 0), (0, 0, 1))),
    ),
    (
        ("P1", ((1, 0, 1), (0, 0, 2))),
        ("M1", ((0, 1, 3), (1, 1, 0))),
        ("X", ((0, 2, 0), (0, 1, 1))),
        ("P2", ((1, 3, 0), (1, 1, 0))),
        ("M2", ((0, 2, 0), (0, 1, 1))),
    ),
    (
        ("P2", ((0, 2, 3),)),
        ("X", ((0, 3, 2),)),
        ("M1", ((1, 0, 2),)),
        ("P1", ((1, 0, 2),)),
        ("M2", ((1, 2, 0),)),
        ("D1", ((1, 0, 2),)),
    ),
)
STEPS = {"P1": (0, 1), "M1": (0, -1), "D1": (0, 2), "P2": (1, 1), "M2": (1, -1)}


def row_of(place):
    return int(np.ravel_multi_index(place, DIMS))


def pairs_of(channel):
    pairs = []
    for place in np.ndindex(*DIMS):
        to = list(place)
        if channel == "X":
            to[2] = 1 - to[2]
        elif channel == "C":
            to[3] = 1 - to[3]
        else:
            axis, by = STEPS[channel]
            axis = (axis + place[2]) % 2
            to[axis] = (to[axis] + by) % DIMS[axis]
        pairs.append((row_of(place), row_of(to)))
    return pairs


def arrived(channel, unit):
    t, a, b = unit
    if channel == "X":
        return (1 - t, b, a)
    axis, by = STEPS[channel]
    return (t, (a - by) % 4, b) if axis == 0 else (t, a, (b - by) % 4)


def send(x, channel):
    return lax.ppermute(x, "row", pairs_of(channel))


def rows_of_units(units, row, core):
    t, a, b = (np.array(v, np.int32) for v in zip(*units))
    z, y, h = row // 16, row // 4 % 4, row // 2 % 2
    z = (z + jnp.where(h == 0, a, b)) % 4
    y = (y + jnp.where(h == 0, b, a)) % 4
    return ((z * 4 + y) * 2 + (h + t) % 2) * 2 + core


def pack_kernel(spots, block, row_ids, codes, counts, *refs):
    arrays, out, sems = refs[:-2], refs[-2], refs[-1]

    def each(act):
        for n, (which, at) in enumerate(spots):
            owner = row_ids[n]
            for k in range(SLOTS):

                @pl.when(k < counts[owner])
                def _():
                    start = pl.multiple_of(at + codes[owner * SLOTS + k] % 4 * block, block)
                    act(
                        pltpu.make_async_copy(
                            arrays[which].at[pl.ds(start, block)], out.at[n * SLOTS + k], sems.at[n * SLOTS + k]
                        )
                    )

    each(lambda copy: copy.start())
    each(lambda copy: copy.wait())


def pack(arrays, spots, row_ids, codes, counts, block):
    channels = arrays[0].shape[1]
    n = len(spots) * SLOTS
    return pl.pallas_call(
        functools.partial(pack_kernel, spots, block),
        out_shape=jax.ShapeDtypeStruct((n, block, channels), jnp.bfloat16),
        in_specs=[pl.BlockSpec(memory_space=pltpu.SMEM)] * 3 + [pl.BlockSpec(memory_space=pl.ANY)] * len(arrays),
        out_specs=pl.BlockSpec(memory_space=pl.ANY),
        scratch_shapes=[pltpu.SemaphoreType.DMA((n,))],
        cost_estimate=pl.CostEstimate(flops=0, bytes_accessed=n * block * channels * 4, transcendentals=0),
        name="pack",
    )(row_ids, codes, counts, *arrays)


def terms_kernel(spots, n_packed, n_arrays, first, last, base, row_ids, codes, counts, blocks, *refs):
    arrays, refs = refs[:n_arrays], refs[n_arrays:]
    if n_packed:
        packed, refs = refs[0], refs[1:]
    if not first:
        total_in, refs = refs[0], refs[1:]
    if last:
        kept, sent, refs = refs[0], refs[1], refs[2:]
        total, refs = refs[0], refs[1:]
    else:
        total, refs = refs[0], refs[1:]
    weights, picked, weight_sems, picked_sems = refs
    block = weights.shape[1]
    n_units = len(spots) + n_packed

    def source(n, k):
        owner = row_ids[n]
        if n < len(spots):
            which, at = spots[n]
            start = pl.multiple_of(at + codes[owner * SLOTS + k] % 4 * block, block)
            return arrays[which].at[pl.ds(start, block)]
        return packed.at[(n - len(spots)) * SLOTS + k]

    for n in range(n_units):
        owner = row_ids[n]
        for k in range(SLOTS):

            @pl.when(k < counts[owner])
            def _():
                task = n * SLOTS + k
                pltpu.make_async_copy(blocks.at[owner, k], weights.at[task], weight_sems.at[task]).start()
                pltpu.make_async_copy(source(n, k), picked.at[task], picked_sems.at[task]).start()

    total[...] = jnp.zeros_like(total) if first else total_in[...]

    def step(task, carry):
        owner = row_ids[task // SLOTS]

        @pl.when(task % SLOTS < counts[owner])
        def _():
            pltpu.make_async_copy(blocks.at[0, 0], weights.at[task], weight_sems.at[task]).wait()
            pltpu.make_async_copy(picked.at[task], picked.at[task], picked_sems.at[task]).wait()
            target = (codes[owner * SLOTS + task % SLOTS] // 4 + base[0]) % 8
            rows = pl.ds(pl.multiple_of(target * block, block), block)
            total[rows, :] += jnp.dot(weights[task], picked[task], preferred_element_type=jnp.float32)

        return carry

    lax.fori_loop(0, n_units * SLOTS, step, 0)
    if last:
        half = kept.shape[0]
        kept[...] = total[:half, :]
        sent[...] = total[half:, :].astype(sent.dtype)


def terms(arrays, spots, packed, row_ids, base, codes, counts, blocks, running, last):
    block = blocks.shape[-1]
    channels = (arrays[0] if arrays else packed).shape[-1]
    n_packed = 0 if packed is None else packed.shape[0] // SLOTS
    n = (len(spots) + n_packed) * SLOTS
    rows = 8 * block
    operands = [base, row_ids, codes, counts, blocks, *arrays]
    specs = [pl.BlockSpec(memory_space=pltpu.SMEM)] * 4 + [pl.BlockSpec(memory_space=pl.ANY)] * (1 + len(arrays))
    if packed is not None:
        operands.append(packed)
        specs.append(pl.BlockSpec(memory_space=pl.ANY))
    if running is not None:
        operands.append(running)
        specs.append(pl.BlockSpec(memory_space=pltpu.VMEM))
    whole = jax.ShapeDtypeStruct((rows, channels), jnp.float32)
    scratch = [
        pltpu.VMEM((n, block, block), jnp.bfloat16),
        pltpu.VMEM((n, block, channels), jnp.bfloat16),
        pltpu.SemaphoreType.DMA((n,)),
        pltpu.SemaphoreType.DMA((n,)),
    ]
    if last:
        shapes = (
            jax.ShapeDtypeStruct((rows // 2, channels), jnp.float32),
            jax.ShapeDtypeStruct((rows // 2, channels), jnp.bfloat16),
        )
        scratch.insert(0, pltpu.VMEM((rows, channels), jnp.float32))
    else:
        shapes = whole
    vmem = pl.BlockSpec(memory_space=pltpu.VMEM)
    return pl.pallas_call(
        functools.partial(terms_kernel, spots, n_packed, len(arrays), running is None, last),
        out_shape=shapes,
        in_specs=specs,
        out_specs=(vmem, vmem) if last else vmem,
        scratch_shapes=scratch,
        compiler_params=pltpu.CompilerParams(vmem_limit_bytes=16 * 2**20),
        cost_estimate=pl.CostEstimate(
            flops=2 * n * block * block * channels,
            bytes_accessed=n * (block * block + block * channels) * 2,
            transcendentals=0,
        ),
        name="terms",
    )(*operands)


def body(features, blocks, codes, counts, weight, bias):
    block = blocks.shape[-1]
    size = features.shape[0]
    row = lax.axis_index("row").astype(jnp.int32)
    core = row % 2
    base = (4 * lax.axis_index("rep").astype(jnp.int32)).reshape(1)
    blocks = blocks.reshape(blocks.shape[2:])
    table = jnp.concatenate([codes.reshape(-1), counts.reshape(-1)])
    other = send(table, "C")
    codes, counts = table[: codes.size], table[codes.size :]
    other_codes, other_counts = other[: codes.size], other[codes.size :]

    held = {HOME: (0, 0)}
    everything = [(features, (HOME,))]
    groups = []
    for number, moves in enumerate(ROUNDS):
        fresh = []
        for channel, units in moves:
            sources = {held[u][0] for u in units}
            if len(sources) == 1 and set(everything[min(sources)][1]) == set(units):
                x, units = everything[min(sources)]
            else:
                x = [everything[held[u][0]][0][held[u][1] * size : (held[u][1] + 1) * size] for u in units]
                x = x[0] if len(x) == 1 else jnp.concatenate(x)
            fresh.append((send(x, channel), tuple(arrived(channel, u) for u in units)))
        group = [everything[0]] if number == 0 else []
        for x, units in fresh:
            for at, u in enumerate(units):
                assert u not in held, u
                held[u] = (len(everything), at)
            everything.append((x, units))
            group.append((x, units))
        groups.append(group)

    running, packed, packed_rows = None, None, None
    for group in groups + [[]]:
        arrays = [x for x, _ in group]
        units = [u for _, us in group for u in us]
        spots = tuple((i, at * size) for i, (_, us) in enumerate(group) for at in range(len(us)))
        ids = [] if not units else [rows_of_units(units, row, core)]
        if packed is not None:
            ids.append(packed_rows)
        ids = ids[0] if len(ids) == 1 else jnp.concatenate(ids)
        following = None
        if units:
            following = send(
                pack(arrays, spots, rows_of_units(units, row, core), other_codes, other_counts, block), "C"
            )
            following_rows = rows_of_units(units, row, 1 - core)
        running = terms(
            arrays, spots, packed, ids, base, codes, counts, blocks, running, not units
        )
        if units:
            packed, packed_rows = following, following_rows
    kept, sent = running
    received = lax.ppermute(sent, "rep", [(0, 1), (1, 0)])
    shares = (kept + received.astype(jnp.float32)).astype(jnp.bfloat16)
    hidden = jnp.dot(shares, weight, preferred_element_type=jnp.float32) + bias
    return jnp.maximum(hidden, 0.0).astype(jnp.bfloat16)


def solution(mesh):
    placed = (
        P(("row", "rep"), None),
        P("row", "rep", None, None, None, None),
        P("row", "rep", None, None),
        P("row", "rep", None),
        P(),
        P(),
    )
    return jax.shard_map(
        body, mesh=mesh, in_specs=placed, out_specs=P(("row", "rep"), None), check_vma=False
    )
```

```python
import functools

import jax
import jax.numpy as jnp
import numpy as np
from jax import lax
from jax.experimental import pallas as pl
from jax.experimental.pallas import tpu as pltpu
from jax.sharding import PartitionSpec as P

DIMS = (4, 4, 2, 2)
SLOTS = 2
VMEM_LIMIT = 4 * 2**20
WIDTH = 2

HOME = (0, 0, 0)
ROUNDS = (
    (("P1", (HOME,)), ("M1", (HOME,)), ("X", (HOME,)), ("P2", (HOME,)), ("M2", (HOME,))),
    (
        ("P1", ((0, 0, 3), (0, 0, 1))),
        ("M1", ((0, 1, 0), (0, 0, 1))),
        ("X", ((0, 0, 3), (0, 0, 1))),
        ("P2", ((1, 0, 0), (0, 1, 0))),
        ("M2", ((1, 0, 0), (0, 0, 1))),
    ),
    (
        ("P1", ((1, 0, 1), (0, 0, 2))),
        ("M1", ((0, 1, 3), (1, 1, 0))),
        ("X", ((0, 2, 0), (0, 1, 1))),
        ("P2", ((1, 3, 0), (1, 1, 0))),
        ("M2", ((0, 2, 0), (0, 1, 1))),
    ),
    (
        ("D1", ((1, 0, 2),)),
        ("P1", ((1, 0, 2),)),
        ("X", ((0, 2, 1),)),
        ("P2", ((0, 2, 3), (1, 2, 0))),
        ("M2", ((1, 2, 0),)),
    ),
)
LATE = ("P2", "M2")
STEPS = {"P1": (0, 1), "M1": (0, -1), "D1": (0, 2), "P2": (1, 1), "M2": (1, -1)}


def row_of(place):
    return int(np.ravel_multi_index(place, DIMS))


def pairs_of(channel):
    pairs = []
    for place in np.ndindex(*DIMS):
        to = list(place)
        if channel == "X":
            to[2] = 1 - to[2]
        elif channel == "C":
            to[3] = 1 - to[3]
        else:
            axis, by = STEPS[channel]
            axis = (axis + place[2]) % 2
            to[axis] = (to[axis] + by * (1 - 2 * place[3])) % DIMS[axis]
        pairs.append((row_of(place), row_of(to)))
    return pairs


def arrived(channel, unit):
    t, a, b = unit
    if channel == "X":
        return (1 - t, b, a)
    axis, by = STEPS[channel]
    return (t, (a - by) % 4, b) if axis == 0 else (t, a, (b - by) % 4)


def send(x, channel):
    return lax.ppermute(x, "row", pairs_of(channel))


def owner_of(where, unit, core_flip):
    t, a, b = unit
    row = where[0]
    h = (row >> 1) & 1
    sign = 1 - 2 * ((row & 1) ^ core_flip)
    a, b = a * sign, b * sign
    z = ((row >> 4) + a + h * (b - a)) & 3
    y = (((row >> 2) & 3) + b + h * (a - b)) & 3
    return (((z * 4 + y) * 2 + (h ^ t)) << 1) + ((row & 1) ^ core_flip)


def pack_kernel(layout, block, where, codes, *refs):
    arrays, out = refs[:-1], refs[-1]
    n = 0
    for array, units in zip(arrays, layout):
        size = array.shape[0] // len(units)
        for at, unit in enumerate(units):
            owner = owner_of(where, unit, 0)
            for k in range(SLOTS):

                @pl.when(k < codes[SLOTS, owner])
                def _():
                    start = pl.multiple_of(at * size + (codes[k, owner] & 3) * block, block)
                    out[n * SLOTS + k] = array[pl.ds(start, block), :]

            n += 1


def pack(arrays, layout, where, codes, block):
    channels = arrays[0].shape[1]
    n = sum(map(len, layout)) * SLOTS
    vmem = pl.BlockSpec(memory_space=pltpu.VMEM)
    return pl.pallas_call(
        functools.partial(pack_kernel, layout, block),
        out_shape=jax.ShapeDtypeStruct((n, block, channels), jnp.bfloat16),
        in_specs=[pl.BlockSpec(memory_space=pltpu.SMEM)] * 2 + [vmem] * len(arrays),
        out_specs=vmem,
        cost_estimate=pl.CostEstimate(flops=0, bytes_accessed=n * block * channels * 4, transcendentals=0),
        compiler_params=pltpu.CompilerParams(vmem_limit_bytes=VMEM_LIMIT),
        name="pack",
    )(where, codes, *arrays)


def terms_kernel(layout, others, first, last, where, codes, blocks, *refs):
    arrays, refs = refs[: len(layout)], refs[len(layout) :]
    if others:
        packed, refs = refs[0], refs[1:]
    if not first:
        total_in, refs = refs[0], refs[1:]
    if last:
        kept, sent, refs = refs[0], refs[1], refs[2:]
    (total,) = refs
    block = blocks.shape[-1]
    units = [(u, 0) for us in layout for u in us] + [(u, 1) for u in others]

    total[...] = jnp.zeros_like(total) if first else total_in[...]
    base = where[1] * 4

    def products(pieces):
        found = []
        for owner, k, features in pieces:
            target = ((codes[k, owner] >> 2) + base) & 7
            rows = pl.ds(pl.multiple_of(target * block, block), block)
            found.append((rows, jnp.dot(blocks[owner, k], features, preferred_element_type=jnp.float32)))
        for rows, product in found:
            total[rows, :] += product

    def sweep(units, flip, features):
        for first in range(0, len(units), WIDTH):
            some = range(first, min(first + WIDTH, len(units)))
            owners = [owner_of(where, units[i], flip) for i in some]
            live = [codes[SLOTS, owner] for owner in owners]

            def pieces(which, slots, some=some, owners=owners):
                return [
                    (owners[n], k, features(some[n], codes[k, owners[n]], k))
                    for n in which
                    for k in range(slots)
                ]

            whole = functools.reduce(jnp.logical_and, [n == SLOTS for n in live])

            @pl.when(whole)
            def _():
                products(pieces(range(len(some)), SLOTS))

            @pl.when(jnp.logical_not(whole))
            def _():
                for n in range(len(some)):
                    for slots in range(1, SLOTS + 1):

                        @pl.when(live[n] == slots)
                        def _():
                            products(pieces([n], slots))

    for array, us in zip(arrays, layout):
        size = array.shape[0] // len(us)

        def features(i, code, k, array=array, size=size):
            return array[pl.ds(pl.multiple_of(i * size + (code & 3) * block, block), block), :]

        sweep(us, 0, features)
    if others:
        sweep(others, 1, lambda i, code, k: packed[i * SLOTS + k])
    if last:
        half = kept.shape[0]
        kept[...] = total[:half, :]
        sent[...] = total[half:, :].astype(sent.dtype)


def terms(arrays, layout, packed, others, where, codes, blocks, running, last):
    block = blocks.shape[-1]
    channels = (arrays[0] if arrays else packed).shape[-1]
    units = sum(map(len, layout)) + len(others)
    n = units * SLOTS
    rows = 8 * block
    vmem = pl.BlockSpec(memory_space=pltpu.VMEM)
    operands = [where, codes, blocks, *arrays]
    specs = [pl.BlockSpec(memory_space=pltpu.SMEM)] * 2 + [vmem] * (1 + len(arrays))
    for extra in (packed, running):
        if extra is not None:
            operands.append(extra)
            specs.append(vmem)
    scratch = []
    if last:
        shapes = (
            jax.ShapeDtypeStruct((rows // 2, channels), jnp.float32),
            jax.ShapeDtypeStruct((rows // 2, channels), jnp.bfloat16),
        )
        scratch.insert(0, pltpu.VMEM((rows, channels), jnp.float32))
    else:
        shapes = jax.ShapeDtypeStruct((rows, channels), jnp.float32)
    return pl.pallas_call(
        functools.partial(terms_kernel, layout, others, running is None, last),
        out_shape=shapes,
        in_specs=specs,
        out_specs=(vmem, vmem) if last else vmem,
        scratch_shapes=scratch,
        compiler_params=pltpu.CompilerParams(vmem_limit_bytes=VMEM_LIMIT),
        cost_estimate=pl.CostEstimate(
            flops=2 * n * block * block * channels,
            bytes_accessed=n * (block * block + block * channels) * 2,
            transcendentals=0,
        ),
        name="terms",
    )(*operands)


def load_kernel(source, out, sem):
    copy = pltpu.make_async_copy(source, out, sem)
    copy.start()
    copy.wait()


def load(blocks):
    return pl.pallas_call(
        load_kernel,
        out_shape=pltpu.VMEM(blocks.shape, blocks.dtype),
        in_specs=[pl.BlockSpec(memory_space=pltpu.HBM)],
        out_specs=pl.BlockSpec(memory_space=pltpu.VMEM),
        scratch_shapes=[pltpu.SemaphoreType.DMA(())],
        compiler_params=pltpu.CompilerParams(vmem_limit_bytes=VMEM_LIMIT),
        cost_estimate=pl.CostEstimate(flops=0, bytes_accessed=2 * blocks.size, transcendentals=0),
        name="load",
    )(pltpu.with_memory_space_constraint(blocks, pltpu.HBM))


def after(xs, *others):
    return list(lax.optimization_barrier((tuple(xs), others))[0])


def body(features, blocks, codes, counts, weight, bias):
    block = blocks.shape[-1]
    size = features.shape[0]
    where = jnp.stack([lax.axis_index("row"), lax.axis_index("rep")]).astype(jnp.int32)
    blocks = blocks.reshape(blocks.shape[2:])
    codes = jnp.concatenate([codes.reshape(codes.shape[2:]).T, counts.reshape(1, -1)])
    other_codes = send(codes, "C")

    held = {HOME: (0, 0)}
    everything = [(features, (HOME,))]
    group = everything[:]
    running, waiting = None, None

    def share(group):
        arrays, layout = [x for x, _ in group], tuple(us for _, us in group)
        packed = pack(arrays, layout, where, other_codes, block)
        return packed, tuple(u for us in layout for u in us)

    def add(group, packed, others, running, last=False):
        arrays, layout = [x for x, _ in group], tuple(us for _, us in group)
        return terms(arrays, layout, packed, others, where, codes, blocks, running, last)

    for number, moves in enumerate(ROUNDS):
        payloads = []
        for channel, units in moves:
            sources = {held[u][0] for u in units}
            if len(sources) == 1 and set(everything[min(sources)][1]) == set(units):
                x, units = everything[min(sources)]
            else:
                x = [everything[held[u][0]][0][held[u][1] * size : (held[u][1] + 1) * size] for u in units]
                x = x[0] if len(x) == 1 else jnp.concatenate(x)
            payloads.append((channel, x, units))
        if number:
            deps = [x for x, _ in group]
            if waiting is not None:
                running = add(*waiting, running)
                deps.append(running)
            else:
                blocks = load(blocks)
                deps.append(blocks)
            xs = after([x for x, _ in group], deps[-1])
            group = [(x, us) for x, (_, us) in zip(xs, group)]
            packed, others = share(group)
            deps.append(packed)
            packed = send(packed, "C")
            waiting = (group, packed, others)
            early = [p for p in payloads if p[0] not in LATE]
            late = [p for p in payloads if p[0] in LATE]
            xs = after([x for _, x, _ in early], *deps) + after([x for _, x, _ in late], *deps, packed)
            payloads = [(channel, x, units) for (channel, _, units), x in zip(early + late, xs)]
        group = group if number == 0 else []
        for channel, x, units in payloads:
            x, units = send(x, channel), tuple(arrived(channel, u) for u in units)
            for at, u in enumerate(units):
                assert u not in held, u
                held[u] = (len(everything), at)
            everything.append((x, units))
            group.append((x, units))
    assert len(held) == 32
    running = add(*waiting, running)
    xs = after([x for x, _ in group], running)
    group = [(x, us) for x, (_, us) in zip(xs, group)]
    packed, others = share(group)
    running = add(group, None, (), running)
    kept, sent = add([], send(packed, "C"), others, running, True)
    received = lax.ppermute(sent, "rep", [(0, 1), (1, 0)])
    shares = (kept + received.astype(jnp.float32)).astype(jnp.bfloat16)
    hidden = jnp.dot(shares, weight, preferred_element_type=jnp.float32) + bias
    return jnp.maximum(hidden, 0.0).astype(jnp.bfloat16)


def solution(mesh):
    placed = (
        P(("row", "rep"), None),
        P("row", "rep", None, None, None, None),
        P("row", "rep", None, None),
        P("row", "rep", None),
        P(),
        P(),
    )
    return jax.shard_map(
        body, mesh=mesh, in_specs=placed, out_specs=P(("row", "rep"), None), check_vma=False
    )
```

```python
import functools

import jax
import jax.numpy as jnp
import numpy as np
from jax import lax
from jax.experimental import pallas as pl
from jax.experimental.pallas import tpu as pltpu
from jax.sharding import PartitionSpec as P

DIMS = (4, 4, 2, 2)
SLOTS = 2
VMEM_LIMIT = 4 * 2**20
WIDTH = 2

HOME = (0, 0, 0)
ROUNDS = (
    (("P1", (HOME,)), ("M1", (HOME,)), ("X", (HOME,)), ("P2", (HOME,)), ("M2", (HOME,))),
    (
        ("P1", ((0, 0, 3), (0, 0, 1))),
        ("M1", ((0, 1, 0), (0, 0, 1))),
        ("X", ((0, 0, 3), (0, 0, 1))),
        ("P2", ((1, 0, 0), (0, 1, 0))),
        ("M2", ((1, 0, 0), (0, 0, 1))),
    ),
    (
        ("P1", ((1, 0, 1), (0, 0, 2))),
        ("M1", ((0, 1, 3), (1, 1, 0))),
        ("X", ((0, 2, 0), (0, 1, 1))),
        ("P2", ((1, 3, 0), (1, 1, 0))),
        ("M2", ((0, 2, 0), (0, 1, 1))),
    ),
    (
        ("D1", ((1, 0, 2),)),
        ("P1", ((1, 0, 2),)),
        ("X", ((0, 2, 1),)),
        ("P2", ((0, 2, 3), (1, 2, 0))),
        ("M2", ((1, 2, 0),)),
    ),
)
LATE = ((), (), ("P2", "M2"), ("M2",))
CLASS = {"P1": 1, "M1": 1, "D1": 1, "X": 0, "P2": 2, "M2": 2}
REUSE = True
OWN = (False, False, False, False)
MIRROR = True
STEPS = {"P1": (0, 1), "M1": (0, -1), "D1": (0, 2), "P2": (1, 1), "M2": (1, -1)}


def row_of(place):
    return int(np.ravel_multi_index(place, DIMS))


def pairs_of(channel):
    pairs = []
    for place in np.ndindex(*DIMS):
        to = list(place)
        if channel == "X":
            to[2] = 1 - to[2]
        elif channel == "C":
            to[3] = 1 - to[3]
        else:
            axis, by = STEPS[channel]
            axis = (axis + place[2]) % 2
            to[axis] = (to[axis] + by * (1 - 2 * place[3] * MIRROR)) % DIMS[axis]
        pairs.append((row_of(place), row_of(to)))
    return pairs


def arrived(channel, unit):
    t, a, b = unit
    if channel == "X":
        return (1 - t, b, a)
    axis, by = STEPS[channel]
    return (t, (a - by) % 4, b) if axis == 0 else (t, a, (b - by) % 4)


def send(x, channel):
    return lax.ppermute(x, "row", pairs_of(channel))


def owner_of(where, unit, core_flip):
    t, a, b = unit
    row = where[0]
    h = (row >> 1) & 1
    sign = 1 - 2 * ((row & 1) ^ core_flip)
    if MIRROR:
        a, b = a * sign, b * sign
    z = ((row >> 4) + a + h * (b - a)) & 3
    y = (((row >> 2) & 3) + b + h * (a - b)) & 3
    return (((z * 4 + y) * 2 + (h ^ t)) << 1) + ((row & 1) ^ core_flip)


def pack_kernel(layout, begin, block, where, codes, *refs):
    arrays, out = refs[: len(layout)], refs[-1]
    n = begin
    for array, units in zip(arrays, layout):
        size = array.shape[0] // len(units)
        for at, unit in enumerate(units):
            owner = owner_of(where, unit, 0)
            for k in range(SLOTS):

                @pl.when(k < codes[SLOTS, owner])
                def _():
                    start = pl.multiple_of(at * size + (codes[k, owner] & 3) * block, block)
                    out[n * SLOTS + k] = array[pl.ds(start, block), :]

            n += 1


def pack(group, where, codes, block, total, into=None):
    arrays, layout = [x for x, _ in group], tuple(us for _, us in group)
    channels = arrays[0].shape[1]
    count = sum(map(len, layout))
    vmem = pl.BlockSpec(memory_space=pltpu.VMEM)
    operands = [where, codes, *arrays] + ([] if into is None else [into])
    return pl.pallas_call(
        functools.partial(pack_kernel, layout, 0 if into is None else total - count, block),
        out_shape=jax.ShapeDtypeStruct((total * SLOTS, block, channels), jnp.bfloat16),
        in_specs=[pl.BlockSpec(memory_space=pltpu.SMEM)] * 2 + [vmem] * (len(operands) - 2),
        out_specs=vmem,
        input_output_aliases={} if into is None else {len(operands) - 1: 0},
        cost_estimate=pl.CostEstimate(
            flops=0, bytes_accessed=count * SLOTS * block * channels * 4, transcendentals=0
        ),
        compiler_params=pltpu.CompilerParams(vmem_limit_bytes=VMEM_LIMIT),
        name="pack",
    )(*operands)


def terms_kernel(layout, others, half, where, codes, blocks, *refs):
    arrays, refs = refs[: len(layout)], refs[len(layout) :]
    packed = total_in = None
    if others:
        packed, refs = refs[0], refs[1:]
    if len(refs) > 1:
        total_in, refs = refs[0], refs[1:]
    (total,) = refs
    block = blocks.shape[-1]
    base = where[1] * 4
    size = total.shape[0]

    if total_in is None:
        total[...] = jnp.zeros_like(total)
    elif total_in.shape == total.shape:
        total[...] = total_in[...]
    else:
        total[...] = total_in[half * size : (half + 1) * size, :]

    def target_of(owner, k):
        return ((codes[k, owner] >> 2) + base) & 7

    def products(pieces):
        found = []
        for owner, k, features in pieces:
            target = target_of(owner, k)
            if half is not None:
                target = target & 3
            rows = pl.ds(pl.multiple_of(target * block, block), block)
            found.append((rows, jnp.dot(blocks[owner, k], features, preferred_element_type=jnp.float32)))
        for rows, product in found:
            total[rows, :] += product

    def sweep(units, flip, features):
        for first in range(0, len(units), WIDTH):
            some = range(first, min(first + WIDTH, len(units)))
            owners = [owner_of(where, units[i], flip) for i in some]
            live = [[k < codes[SLOTS, owner] for k in range(SLOTS)] for owner in owners]
            if half is not None:
                live = [
                    [on & (target_of(owner, k) >> 2 == half) for k, on in enumerate(ons)]
                    for owner, ons in zip(owners, live)
                ]

            def pieces(which, some=some, owners=owners):
                return [(owners[n], k, features(some[n], codes[k, owners[n]], k)) for n, k in which]

            def branch(which, condition):
                pl.when(condition)(lambda: products(pieces(which)))

            pairs = [functools.reduce(jnp.logical_and, ons) for ons in live]
            if half is not None:
                for n, (ons, pair) in enumerate(zip(live, pairs)):
                    branch([(n, k) for k in range(SLOTS)], pair)
                    for k, on in enumerate(ons):
                        branch([(n, k)], on & jnp.logical_not(pair))
                continue
            whole = functools.reduce(jnp.logical_and, pairs)
            branch([(n, k) for n in range(len(some)) for k in range(SLOTS)], whole)

            @pl.when(jnp.logical_not(whole))
            def _():
                for n, owner in enumerate(owners):
                    for slots in range(1, SLOTS + 1):
                        branch([(n, k) for k in range(slots)], codes[SLOTS, owner] == slots)

    for array, us in zip(arrays, layout):
        unit_rows = array.shape[0] // len(us)

        def features(i, code, k, array=array, unit_rows=unit_rows):
            return array[pl.ds(pl.multiple_of(i * unit_rows + (code & 3) * block, block), block), :]

        sweep(us, 0, features)
    if others:
        sweep(others, 1, lambda i, code, k: packed[i * SLOTS + k])


def terms(group, packed, others, running, where, codes, blocks, half=None):
    arrays, layout = [x for x, _ in group], tuple(us for _, us in group)
    block = blocks.shape[-1]
    channels = (arrays[0] if arrays else packed).shape[-1]
    n = (sum(map(len, layout)) + len(others)) * SLOTS
    vmem = pl.BlockSpec(memory_space=pltpu.VMEM)
    operands = [where, codes, blocks, *arrays]
    operands += [x for x in (packed, running) if x is not None]
    return pl.pallas_call(
        functools.partial(terms_kernel, layout, others, half),
        out_shape=jax.ShapeDtypeStruct((8 * block if half is None else 4 * block, channels), jnp.float32),
        in_specs=[pl.BlockSpec(memory_space=pltpu.SMEM)] * 2 + [vmem] * (len(operands) - 2),
        out_specs=vmem,
        compiler_params=pltpu.CompilerParams(vmem_limit_bytes=VMEM_LIMIT),
        cost_estimate=pl.CostEstimate(
            flops=2 * n * block * block * channels,
            bytes_accessed=n * (block * block + block * channels) * 2,
            transcendentals=0,
        ),
        name="terms",
    )(*operands)


def load_kernel(source, out, sem):
    copy = pltpu.make_async_copy(source, out, sem)
    copy.start()
    copy.wait()


def load(blocks):
    return pl.pallas_call(
        load_kernel,
        out_shape=pltpu.VMEM(blocks.shape, blocks.dtype),
        in_specs=[pl.BlockSpec(memory_space=pltpu.HBM)],
        out_specs=pl.BlockSpec(memory_space=pltpu.VMEM),
        scratch_shapes=[pltpu.SemaphoreType.DMA(())],
        compiler_params=pltpu.CompilerParams(vmem_limit_bytes=VMEM_LIMIT),
        cost_estimate=pl.CostEstimate(flops=0, bytes_accessed=2 * blocks.size, transcendentals=0),
        name="load",
    )(pltpu.with_memory_space_constraint(blocks, pltpu.HBM))


def after(xs, *others):
    return list(lax.optimization_barrier((tuple(xs), others))[0])


def body(features, blocks, codes, counts, weight, bias):
    block = blocks.shape[-1]
    size = features.shape[0]
    where = jnp.stack([lax.axis_index("row"), lax.axis_index("rep")]).astype(jnp.int32)
    blocks = blocks.reshape(blocks.shape[2:])
    codes = jnp.concatenate([codes.reshape(codes.shape[2:]).T, counts.reshape(1, -1)])
    other_codes = send(codes, "C")

    held = {HOME: (0, 0)}
    everything = [(features, (HOME,))]
    group = everything[:]
    running, waiting = None, None

    def add(group, packed, others, running, half=None):
        return terms(group, packed, others, running, where, codes, blocks, half)

    for number, moves in enumerate(ROUNDS):
        payloads = []
        for channel, units in moves:
            sources = {held[u][0] for u in units}
            if len(sources) == 1 and set(everything[min(sources)][1]) == set(units):
                x, units = everything[min(sources)]
            else:
                x = [everything[held[u][0]][0][held[u][1] * size : (held[u][1] + 1) * size] for u in units]
                x = x[0] if len(x) == 1 else jnp.concatenate(x)
            payloads.append((channel, x, units))
        if number:
            deps, packed, others = [], None, ()
            if number == 1 and REUSE:
                found = {c: (x, us) for c, x, us in payloads}
                first = [everything[0]]
                have = {HOME}
                for c, x, us in payloads + [(None, x, us) for x, us in group]:
                    if not have & set(us):
                        first.append((x, us))
                        have |= set(us)
                shared = first
            elif number == 1:
                shared = group
            if number >= 2:
                if number == 2:
                    blocks = load(blocks)
                    count = sum(len(us) for _, us in shared + group)
                    into = pack(shared, where, other_codes, block, count)
                running = add(*waiting, running)
                xs = after([x for x, _ in group], running, *([into] if number == 2 else []))
                group = [(x, us) for x, (_, us) in zip(xs, group)]
                others = tuple(u for _, us in group for u in us)
                if number == 2:
                    packed = pack(group, where, other_codes, block, count, into)
                    others = tuple(u for _, us in shared for u in us) + others
                else:
                    packed = pack(group, where, other_codes, block, len(others))
                deps += [running, packed]
                packed = send(packed, "C")
            waiting = (shared if number == 1 else group, packed, others)
            tied = {c: [x for (x, _), k in zip(group[-len(order) :], order) if not OWN[number] or CLASS[k] == CLASS[c]] for c in CLASS}
            early = [p for p in payloads if p[0] not in LATE[number]]
            late = [p for p in payloads if p[0] in LATE[number]]
            xs = [after([x], *tied[c], *deps)[0] for c, x, _ in early]
            xs += [after([x], *tied[c], *deps, *([packed] if number > 1 else []))[0] for c, x, _ in late]
            payloads = [(channel, x, units) for (channel, _, units), x in zip(early + late, xs)]
        group = group if number == 0 else []
        order = [channel for channel, _, _ in payloads]
        for channel, x, units in payloads:
            x, units = send(x, channel), tuple(arrived(channel, u) for u in units)
            for at, u in enumerate(units):
                assert u not in held, u
                held[u] = (len(everything), at)
            everything.append((x, units))
            group.append((x, units))
    assert len(held) == 32
    running = add(*waiting, running)
    xs = after([x for x, _ in group], running)
    group = [(x, us) for x, (_, us) in zip(xs, group)]
    others = tuple(u for _, us in group for u in us)
    packed = send(pack(group, where, other_codes, block, len(others)), "C")
    sent = add(group, None, (), running, 1)
    sent = add([], packed, others, sent, 1)
    kept = add(group, packed, others, running, 0)
    received = lax.ppermute(sent.astype(jnp.bfloat16), "rep", [(0, 1), (1, 0)])
    shares = (kept + received.astype(jnp.float32)).astype(jnp.bfloat16)
    hidden = jnp.dot(shares, weight, preferred_element_type=jnp.float32) + bias
    return jnp.maximum(hidden, 0.0).astype(jnp.bfloat16)


def solution(mesh):
    placed = (
        P(("row", "rep"), None),
        P("row", "rep", None, None, None, None),
        P("row", "rep", None, None),
        P("row", "rep", None),
        P(),
        P(),
    )
    return jax.shard_map(
        body, mesh=mesh, in_specs=placed, out_specs=P(("row", "rep"), None), check_vma=False
    )
```

```python
import functools

import jax
import jax.numpy as jnp
import numpy as np
from jax import lax
from jax.experimental import pallas as pl
from jax.experimental.pallas import tpu as pltpu
from jax.sharding import PartitionSpec as P

DIMS = (4, 4, 2, 2)
SLOTS = 2
VMEM_LIMIT = 4 * 2**20
WIDTH = (2, 4)

HOME = (0, 0, 0)
ROUNDS = (
    (("P1", (HOME,)), ("M1", (HOME,)), ("X", (HOME,)), ("P2", (HOME,)), ("M2", (HOME,))),
    (
        ("P1", ((0, 0, 3), (0, 0, 1))),
        ("M1", ((0, 1, 0), (0, 0, 1))),
        ("X", ((0, 0, 3), (0, 0, 1))),
        ("P2", ((1, 0, 0), (0, 1, 0))),
        ("M2", ((1, 0, 0), (0, 0, 1))),
    ),
    (
        ("P1", ((1, 0, 1), (0, 0, 2))),
        ("M1", ((0, 1, 3), (1, 1, 0))),
        ("X", ((0, 2, 0), (0, 1, 1))),
        ("P2", ((1, 3, 0), (1, 1, 0))),
        ("M2", ((0, 2, 0), (0, 1, 1))),
    ),
    (
        ("D1", ((1, 0, 2),)),
        ("P1", ((1, 0, 2),)),
        ("X", ((0, 2, 1),)),
        ("P2", ((0, 2, 3), (1, 2, 0))),
        ("M2", ((1, 2, 0),)),
    ),
)
MIRROR = True
LATE = ((), (), ('P1', 'P2'), ('M2',))
STEPS = {"P1": (0, 1), "M1": (0, -1), "D1": (0, 2), "P2": (1, 1), "M2": (1, -1)}


def row_of(place):
    return int(np.ravel_multi_index(place, DIMS))


def pairs_of(channel):
    pairs = []
    for place in np.ndindex(*DIMS):
        to = list(place)
        if channel == "X":
            to[2] = 1 - to[2]
        elif channel == "C":
            to[3] = 1 - to[3]
        else:
            axis, by = STEPS[channel]
            axis = (axis + place[2]) % 2
            to[axis] = (to[axis] + by * (1 - 2 * place[3] * MIRROR)) % DIMS[axis]
        pairs.append((row_of(place), row_of(to)))
    return pairs


def arrived(channel, unit):
    t, a, b = unit
    if channel == "X":
        return (1 - t, b, a)
    axis, by = STEPS[channel]
    return (t, (a - by) % 4, b) if axis == 0 else (t, a, (b - by) % 4)


def send(x, channel):
    return lax.ppermute(x, "row", pairs_of(channel))


def owner_of(where, unit, core_flip):
    t, a, b = unit
    row = where[0]
    h = (row >> 1) & 1
    sign = 1 - 2 * ((row & 1) ^ core_flip)
    if MIRROR:
        a, b = a * sign, b * sign
    z = ((row >> 4) + a + h * (b - a)) & 3
    y = (((row >> 2) & 3) + b + h * (a - b)) & 3
    return (((z * 4 + y) * 2 + (h ^ t)) << 1) + ((row & 1) ^ core_flip)


def pack_kernel(layout, begin, block, where, codes, *refs):
    arrays, out = refs[: len(layout)], refs[-1]
    n = begin
    for array, units in zip(arrays, layout):
        size = array.shape[0] // len(units)
        for at, unit in enumerate(units):
            owner = owner_of(where, unit, 0)
            for k in range(SLOTS):

                @pl.when(k < codes[SLOTS, owner])
                def _():
                    start = pl.multiple_of(at * size + (codes[k, owner] & 3) * block, block)
                    out[n * SLOTS + k] = array[pl.ds(start, block), :]

            n += 1


def pack(group, where, codes, block, total, into=None):
    arrays, layout = [x for x, _ in group], tuple(us for _, us in group)
    channels = arrays[0].shape[1]
    count = sum(map(len, layout))
    vmem = pl.BlockSpec(memory_space=pltpu.VMEM)
    operands = [where, codes, *arrays] + ([] if into is None else [into])
    return pl.pallas_call(
        functools.partial(pack_kernel, layout, 0 if into is None else total - count, block),
        out_shape=jax.ShapeDtypeStruct((total * SLOTS, block, channels), jnp.bfloat16),
        in_specs=[pl.BlockSpec(memory_space=pltpu.SMEM)] * 2 + [vmem] * (len(operands) - 2),
        out_specs=vmem,
        input_output_aliases={} if into is None else {len(operands) - 1: 0},
        cost_estimate=pl.CostEstimate(
            flops=0, bytes_accessed=count * SLOTS * block * channels * 4, transcendentals=0
        ),
        compiler_params=pltpu.CompilerParams(vmem_limit_bytes=VMEM_LIMIT),
        name="pack",
    )(*operands)


def terms_kernel(layout, half, where, codes, blocks, *refs):
    arrays, refs = refs[: len(layout)], refs[len(layout) :]
    total_in = None
    if len(refs) > 2:
        total_in, refs = refs[0], refs[1:]
    total, owners = refs
    block = blocks.shape[-1]
    base = where[1] * 4
    size = total.shape[0]

    for n, (unit, flip) in enumerate([(u, flip) for us, flip in layout for u in us]):
        owners[n] = owner_of(where, unit, flip)
    if total_in is None:
        total[...] = jnp.zeros_like(total)
    elif total_in.shape == total.shape:
        total[...] = total_in[...]
    else:
        total[...] = total_in[half * size : (half + 1) * size, :]

    def target_of(owner, k):
        return ((codes[k, owner] >> 2) + base) & 7

    def counts(owner, k):
        live = k < codes[SLOTS, owner]
        return live if half is None else live & (target_of(owner, k) >> 2 == half)

    def sweep(begin, count, features, width):
        def products(tasks):
            found = []
            for i, k in tasks:
                owner = owners[begin + i]
                target = target_of(owner, k)
                if half is not None:
                    target = target & 3
                rows = pl.ds(pl.multiple_of(target * block, block), block)
                product = jnp.dot(
                    blocks[owner, k], features(i, codes[k, owner], k), preferred_element_type=jnp.float32
                )
                found.append((rows, product))
            for rows, product in found:
                total[rows, :] += product

        def some(first, units):
            tasks = [(first + i, k) for i in range(units) for k in range(SLOTS)]
            whole = functools.reduce(jnp.logical_and, [counts(owners[begin + i], k) for i, k in tasks])

            @pl.when(whole)
            def _():
                products(tasks)

            @pl.when(jnp.logical_not(whole))
            def _():
                def one(task, carry):
                    i, k = first + task // SLOTS, task % SLOTS

                    @pl.when(counts(owners[begin + i], k))
                    def _():
                        products([(i, k)])

                    return carry

                lax.fori_loop(0, len(tasks), one, 0)

        width = min(count, width if half is None else 1)
        steps = count // width
        if steps == 1:
            some(0, width)
        elif steps:

            def step(n, carry):
                some(n * width, width)
                return carry

            lax.fori_loop(0, steps, step, 0)
        if count % width:
            some(steps * width, count % width)

    begin = 0
    for array, (us, flip) in zip(arrays, layout):
        unit_rows = array.shape[0] // len(us)

        def features(i, code, k, array=array, unit_rows=unit_rows, flip=flip):
            if flip:
                return array[i * SLOTS + k]
            return array[pl.ds(pl.multiple_of(i * unit_rows + (code & 3) * block, block), block), :]

        sweep(begin, len(us), features, WIDTH[flip])
        begin += len(us)


def terms(group, packed, running, where, codes, blocks, half=None):
    sources = [(x, us, 0) for x, us in group] + [(x, us, 1) for x, us in packed]
    layout = tuple((us, flip) for _, us, flip in sources)
    block = blocks.shape[-1]
    channels = sources[0][0].shape[-1]
    n = sum(len(us) for us, _ in layout) * SLOTS
    vmem = pl.BlockSpec(memory_space=pltpu.VMEM)
    operands = [where, codes, blocks] + [x for x, _, _ in sources] + ([] if running is None else [running])
    return pl.pallas_call(
        functools.partial(terms_kernel, layout, half),
        out_shape=jax.ShapeDtypeStruct((8 * block if half is None else 4 * block, channels), jnp.float32),
        in_specs=[pl.BlockSpec(memory_space=pltpu.SMEM)] * 2 + [vmem] * (len(operands) - 2),
        out_specs=vmem,
        scratch_shapes=[pltpu.SMEM((n // SLOTS,), jnp.int32)],
        compiler_params=pltpu.CompilerParams(vmem_limit_bytes=VMEM_LIMIT),
        cost_estimate=pl.CostEstimate(
            flops=2 * n * block * block * channels,
            bytes_accessed=n * (block * block + block * channels) * 2,
            transcendentals=0,
        ),
        name="terms",
    )(*operands)


def load_kernel(source, out, sem):
    copy = pltpu.make_async_copy(source, out, sem)
    copy.start()
    copy.wait()


def load(blocks):
    return pl.pallas_call(
        load_kernel,
        out_shape=pltpu.VMEM(blocks.shape, blocks.dtype),
        in_specs=[pl.BlockSpec(memory_space=pltpu.HBM)],
        out_specs=pl.BlockSpec(memory_space=pltpu.VMEM),
        scratch_shapes=[pltpu.SemaphoreType.DMA(())],
        compiler_params=pltpu.CompilerParams(vmem_limit_bytes=VMEM_LIMIT),
        cost_estimate=pl.CostEstimate(flops=0, bytes_accessed=2 * blocks.size, transcendentals=0),
        name="load",
    )(pltpu.with_memory_space_constraint(blocks, pltpu.HBM))


def after(xs, *others):
    return list(lax.optimization_barrier((tuple(xs), others))[0])


def body(features, blocks, codes, counts, weight, bias):
    block = blocks.shape[-1]
    size = features.shape[0]
    where = jnp.stack([lax.axis_index("row"), lax.axis_index("rep")]).astype(jnp.int32)
    blocks = blocks.reshape(blocks.shape[2:])
    codes = jnp.concatenate([codes.reshape(codes.shape[2:]).T, counts.reshape(1, -1)])
    other_codes = send(codes, "C")
    held = {HOME: (features, 0)}
    arrays = [(features, (HOME,))]

    def payload(units):
        for x, us in arrays:
            if set(us) == set(units):
                return x, us
        x = [held[u][0][held[u][1] * size : (held[u][1] + 1) * size] for u in units]
        return x[0] if len(x) == 1 else jnp.concatenate(x), units

    def exchange(number, payloads, late, first, second):
        group = []
        payloads = [p for p in payloads if p[0] not in late] + [p for p in payloads if p[0] in late]
        for channel, x, units in payloads:
            x = after([x], *first, *(second if channel in late else ()))[0] if first else x
            x, units = send(x, channel), tuple(arrived(channel, u) for u in units)
            for at, u in enumerate(units):
                assert u not in held, u
                held[u] = (x, at)
            group.append((x, units))
        arrays.extend(group)
        return group

    def names(group):
        return tuple(u for _, us in group for u in us)

    def hold(group, *others):
        return [(x, us) for x, (_, us) in zip(after([x for x, _ in group], *others), group)]

    def payloads(number):
        return [(c,) + payload(us) for c, us in ROUNDS[number]]

    def xs(group):
        return [x for x, _ in group]

    def add(group, packed, running, half=None):
        return terms(group, packed, running, where, codes, blocks, half)

    group = exchange(0, payloads(0), (), (), ())

    moves = payloads(1)
    early, have = [], set()
    for x, us in [(features, (HOME,))] + [(x, us) for _, x, us in moves] + group:
        if not have & set(us):
            early.append((x, us))
            have |= set(us)
    group = exchange(1, moves, (), [*xs(group), other_codes], ())
    blocks = load(blocks)
    count = len(names(early)) + len(names(group))
    packed = pack(early, where, other_codes, block, count)

    moves = payloads(2)
    group = hold(group, packed, blocks)
    packed = pack(group, where, other_codes, block, count, packed)
    first = xs(group) + [packed]
    ready = early + group
    packed = [(send(packed, "C"), names(ready))]
    group = exchange(2, moves, LATE[2], first, xs(packed))
    running = add(ready, packed, None)

    moves = payloads(3)
    group = hold(group, running)
    packed = pack(group, where, other_codes, block, len(names(group)))
    first = xs(group) + [packed]
    ready = group
    packed = [(send(packed, "C"), names(group))]
    group = exchange(3, moves, LATE[3], first, xs(packed))
    running = add(ready, packed, running)

    group = hold(group, running)
    packed = pack(group, where, other_codes, block, len(names(group)))
    packed = [(send(packed, "C"), names(group))]
    sent = add(group, [], running, 1)
    sent = add([], packed, sent, 1)
    kept = add(group, packed, running, 0)
    received = lax.ppermute(sent.astype(jnp.bfloat16), "rep", [(0, 1), (1, 0)])
    shares = (kept + received.astype(jnp.float32)).astype(jnp.bfloat16)
    hidden = jnp.dot(shares, weight, preferred_element_type=jnp.float32) + bias
    return jnp.maximum(hidden, 0.0).astype(jnp.bfloat16)


def solution(mesh):
    placed = (
        P(("row", "rep"), None),
        P("row", "rep", None, None, None, None),
        P("row", "rep", None, None),
        P("row", "rep", None),
        P(),
        P(),
    )
    return jax.shard_map(
        body, mesh=mesh, in_specs=placed, out_specs=P(("row", "rep"), None), check_vma=False
    )
```

```python
import functools

import jax
import jax.numpy as jnp
import numpy as np
from jax import lax
from jax.experimental import pallas as pl
from jax.experimental.pallas import tpu as pltpu
from jax.sharding import PartitionSpec as P

DIMS = (4, 4, 2, 2)
SLOTS = 2
VMEM_LIMIT = 4 * 2**20

HOME = (0, 0, 0)
ROUNDS = (
    (
        ("P2", (HOME,)),
        ("M1", (HOME,)),
        ("P1", (HOME,)),
        ("X", (HOME,)),
        ("M2", (HOME,)),
    ),
    (
        ("M1", ((1, 0, 0), (0, 0, 3))),
        ("X", ((0, 0, 3), (0, 1, 0))),
        ("P2", ((0, 3, 0), (1, 0, 0))),
        ("P1", ((0, 0, 1), (0, 3, 0))),
        ("M2", ((0, 1, 0), (0, 0, 1))),
    ),
    (
        ("M2", ((1, 3, 0), (1, 0, 1))),
        ("P2", ((0, 3, 3), (0, 1, 3))),
        ("X", ((0, 0, 2), (0, 1, 1))),
        ("M1", ((0, 1, 1), (1, 0, 3))),
        ("P1", ((0, 3, 3), (1, 0, 3))),
    ),
    (
        ("M1", ((0, 1, 2),)),
        ("M2", ((1, 2, 0), (1, 3, 1))),
        ("X", ((0, 2, 1),)),
        ("D1", ((1, 0, 2),)),
        ("P2", ((1, 2, 0),)),
    ),
)
LATE = ((), (), ("P1", "P2"), ("P2",))
WIDTH = (2, 4)
STEPS = {"P1": (0, 1), "M1": (0, -1), "D1": (0, 2), "D2": (1, 2), "P2": (1, 1), "M2": (1, -1)}


def row_of(place):
    return int(np.ravel_multi_index(place, DIMS))


def pairs_of(channel):
    pairs = []
    for place in np.ndindex(*DIMS):
        to = list(place)
        if channel == "X":
            to[2] = 1 - to[2]
        elif channel == "C":
            to[3] = 1 - to[3]
        else:
            axis, by = STEPS[channel]
            axis = (axis + place[2]) % 2
            to[axis] = (to[axis] + by * (1 - 2 * place[3])) % DIMS[axis]
        pairs.append((row_of(place), row_of(to)))
    return pairs


def arrived(channel, unit):
    t, a, b = unit
    if channel == "X":
        return (1 - t, b, a)
    axis, by = STEPS[channel]
    return (t, (a - by) % 4, b) if axis == 0 else (t, a, (b - by) % 4)


def send(x, channel):
    return lax.ppermute(x, "row", pairs_of(channel))


def owner_of(where, unit, core_flip):
    t, a, b = unit
    row = where[0]
    h = (row >> 1) & 1
    sign = 1 - 2 * ((row & 1) ^ core_flip)
    a, b = a * sign, b * sign
    z = ((row >> 4) + a + h * (b - a)) & 3
    y = (((row >> 2) & 3) + b + h * (a - b)) & 3
    return (((z * 4 + y) * 2 + (h ^ t)) << 1) + ((row & 1) ^ core_flip)


def pack_kernel(layout, begin, block, where, codes, *refs):
    arrays, out = refs[: len(layout)], refs[-1]
    n = begin
    for array, units in zip(arrays, layout):
        size = array.shape[0] // len(units)
        for at, unit in enumerate(units):
            owner = owner_of(where, unit, 0)
            for k in range(SLOTS):

                @pl.when(k < codes[SLOTS, owner])
                def _():
                    start = pl.multiple_of(at * size + (codes[k, owner] & 3) * block, block)
                    out[n * SLOTS + k] = array[pl.ds(start, block), :]

            n += 1


def pack(group, where, codes, block, total, into=None):
    arrays, layout = [x for x, _ in group], tuple(us for _, us in group)
    channels = arrays[0].shape[1]
    count = sum(map(len, layout))
    vmem = pl.BlockSpec(memory_space=pltpu.VMEM)
    operands = [where, codes, *arrays] + ([] if into is None else [into])
    return pl.pallas_call(
        functools.partial(pack_kernel, layout, 0 if into is None else total - count, block),
        out_shape=jax.ShapeDtypeStruct((total * SLOTS, block, channels), jnp.bfloat16),
        in_specs=[pl.BlockSpec(memory_space=pltpu.SMEM)] * 2 + [vmem] * (len(operands) - 2),
        out_specs=vmem,
        input_output_aliases={} if into is None else {len(operands) - 1: 0},
        cost_estimate=pl.CostEstimate(
            flops=0, bytes_accessed=count * SLOTS * block * channels * 4, transcendentals=0
        ),
        compiler_params=pltpu.CompilerParams(vmem_limit_bytes=VMEM_LIMIT),
        name="pack",
    )(*operands)


def terms_kernel(layout, half, where, codes, blocks, *refs):
    arrays, refs = refs[: len(layout)], refs[len(layout) :]
    total_in = None
    if len(refs) > 2:
        total_in, refs = refs[0], refs[1:]
    total, owners = refs
    block = blocks.shape[-1]
    base = where[1] * 4
    size = total.shape[0]

    for n, (unit, flip) in enumerate([(u, flip) for us, flip in layout for u in us]):
        owners[n] = owner_of(where, unit, flip)
    if total_in is None:
        total[...] = jnp.zeros_like(total)
    elif total_in.shape == total.shape:
        total[...] = total_in[...]
    else:
        total[...] = total_in[half * size : (half + 1) * size, :]

    def target_of(owner, k):
        return ((codes[k, owner] >> 2) + base) & 7

    def counts(owner, k):
        live = k < codes[SLOTS, owner]
        return live if half is None else live & (target_of(owner, k) >> 2 == half)

    def sweep(begin, count, features, width):
        def products(tasks):
            found = []
            for i, k in tasks:
                owner = owners[begin + i]
                target = target_of(owner, k)
                if half is not None:
                    target = target & 3
                rows = pl.ds(pl.multiple_of(target * block, block), block)
                product = jnp.dot(
                    blocks[owner, k], features(i, codes[k, owner], k), preferred_element_type=jnp.float32
                )
                found.append((rows, product))
            for rows, product in found:
                total[rows, :] += product

        def some(first, units):
            tasks = [(first + i, k) for i in range(units) for k in range(SLOTS)]
            whole = functools.reduce(jnp.logical_and, [counts(owners[begin + i], k) for i, k in tasks])

            @pl.when(whole)
            def _():
                products(tasks)

            @pl.when(jnp.logical_not(whole))
            def _():
                def one(task, carry):
                    i, k = first + task // SLOTS, task % SLOTS

                    @pl.when(counts(owners[begin + i], k))
                    def _():
                        products([(i, k)])

                    return carry

                lax.fori_loop(0, len(tasks), one, 0)

        width = min(count, width if half is None else 1)
        steps = count // width
        if steps == 1:
            some(0, width)
        elif steps:

            def step(n, carry):
                some(n * width, width)
                return carry

            lax.fori_loop(0, steps, step, 0)
        if count % width:
            some(steps * width, count % width)

    begin = 0
    for array, (us, flip) in zip(arrays, layout):
        unit_rows = array.shape[0] // len(us)

        def features(i, code, k, array=array, unit_rows=unit_rows, flip=flip):
            if flip:
                return array[i * SLOTS + k]
            return array[pl.ds(pl.multiple_of(i * unit_rows + (code & 3) * block, block), block), :]

        sweep(begin, len(us), features, WIDTH[flip])
        begin += len(us)


def terms(group, packed, running, where, codes, blocks, half=None):
    sources = [(x, us, 0) for x, us in group] + [(x, us, 1) for x, us in packed]
    layout = tuple((us, flip) for _, us, flip in sources)
    block = blocks.shape[-1]
    channels = sources[0][0].shape[-1]
    n = sum(len(us) for us, _ in layout) * SLOTS
    vmem = pl.BlockSpec(memory_space=pltpu.VMEM)
    operands = [where, codes, blocks] + [x for x, _, _ in sources] + ([] if running is None else [running])
    return pl.pallas_call(
        functools.partial(terms_kernel, layout, half),
        out_shape=jax.ShapeDtypeStruct((8 * block if half is None else 4 * block, channels), jnp.float32),
        in_specs=[pl.BlockSpec(memory_space=pltpu.SMEM)] * 2 + [vmem] * (len(operands) - 2),
        out_specs=vmem,
        scratch_shapes=[pltpu.SMEM((n // SLOTS,), jnp.int32)],
        compiler_params=pltpu.CompilerParams(vmem_limit_bytes=VMEM_LIMIT),
        cost_estimate=pl.CostEstimate(
            flops=2 * n * block * block * channels,
            bytes_accessed=n * (block * block + block * channels) * 2,
            transcendentals=0,
        ),
        name="terms",
    )(*operands)


def load_kernel(source, out, sem):
    copy = pltpu.make_async_copy(source, out, sem)
    copy.start()
    copy.wait()


def load(blocks):
    return pl.pallas_call(
        load_kernel,
        out_shape=pltpu.VMEM(blocks.shape, blocks.dtype),
        in_specs=[pl.BlockSpec(memory_space=pltpu.HBM)],
        out_specs=pl.BlockSpec(memory_space=pltpu.VMEM),
        scratch_shapes=[pltpu.SemaphoreType.DMA(())],
        compiler_params=pltpu.CompilerParams(vmem_limit_bytes=VMEM_LIMIT),
        cost_estimate=pl.CostEstimate(flops=0, bytes_accessed=2 * blocks.size, transcendentals=0),
        name="load",
    )(pltpu.with_memory_space_constraint(blocks, pltpu.HBM))


def after(xs, *others):
    return list(lax.optimization_barrier((tuple(xs), others))[0])


def body(features, blocks, codes, counts, weight, bias):
    block = blocks.shape[-1]
    size = features.shape[0]
    where = jnp.stack([lax.axis_index("row"), lax.axis_index("rep")]).astype(jnp.int32)
    blocks = blocks.reshape(blocks.shape[2:])
    codes = jnp.concatenate([codes.reshape(codes.shape[2:]).T, counts.reshape(1, -1)])
    other_codes = send(codes, "C")
    held = {HOME: (features, 0)}
    arrays = [(features, (HOME,))]

    def payload(units):
        for x, us in arrays:
            if set(us) == set(units):
                return x, us
        x = [held[u][0][held[u][1] * size : (held[u][1] + 1) * size] for u in units]
        return x[0] if len(x) == 1 else jnp.concatenate(x), units

    def exchange(number, payloads, late, first, second):
        group = []
        payloads = [p for p in payloads if p[0] not in late] + [p for p in payloads if p[0] in late]
        for channel, x, units in payloads:
            x = after([x], *first, *(second if channel in late else ()))[0] if first else x
            x, units = send(x, channel), tuple(arrived(channel, u) for u in units)
            for at, u in enumerate(units):
                assert u not in held, u
                held[u] = (x, at)
            group.append((x, units))
        arrays.extend(group)
        return group

    def names(group):
        return tuple(u for _, us in group for u in us)

    def hold(group, *others):
        return [(x, us) for x, (_, us) in zip(after([x for x, _ in group], *others), group)]

    def payloads(number):
        return [(c,) + payload(us) for c, us in ROUNDS[number]]

    def xs(group):
        return [x for x, _ in group]

    def add(group, packed, running, half=None):
        return terms(group, packed, running, where, codes, blocks, half)

    group = exchange(0, payloads(0), (), (), ())

    moves = payloads(1)
    early, have = [], set()
    for x, us in [(features, (HOME,))] + [(x, us) for _, x, us in moves] + group:
        if not have & set(us):
            early.append((x, us))
            have |= set(us)
    group = exchange(1, moves, (), [*xs(group), other_codes], ())
    blocks = load(blocks)
    count = len(names(early)) + len(names(group))
    packed = pack(early, where, other_codes, block, count)

    moves = payloads(2)
    group = hold(group, packed, blocks)
    packed = pack(group, where, other_codes, block, count, packed)
    first = xs(group) + [packed]
    ready = early + group
    packed = [(send(packed, "C"), names(ready))]
    group = exchange(2, moves, LATE[2], first, xs(packed))
    running = add(ready, packed, None)

    moves = payloads(3)
    group = hold(group, running)
    packed = pack(group, where, other_codes, block, len(names(group)))
    first = xs(group) + [packed]
    ready = group
    packed = [(send(packed, "C"), names(group))]
    group = exchange(3, moves, LATE[3], first, xs(packed))
    running = add(ready, packed, running)

    group = hold(group, running)
    packed = pack(group, where, other_codes, block, len(names(group)))
    packed = [(send(packed, "C"), names(group))]
    sent = add(group, [], running, 1)
    sent = add([], packed, sent, 1)
    kept = add(group, packed, running, 0)
    received = lax.ppermute(sent.astype(jnp.bfloat16), "rep", [(0, 1), (1, 0)])
    shares = (kept + received.astype(jnp.float32)).astype(jnp.bfloat16)
    hidden = jnp.dot(shares, weight, preferred_element_type=jnp.float32) + bias
    return jnp.maximum(hidden, 0.0).astype(jnp.bfloat16)


def solution(mesh):
    placed = (
        P(("row", "rep"), None),
        P("row", "rep", None, None, None, None),
        P("row", "rep", None, None),
        P("row", "rep", None),
        P(),
        P(),
    )
    return jax.shard_map(
        body, mesh=mesh, in_specs=placed, out_specs=P(("row", "rep"), None), check_vma=False
    )
```

```python
import functools

import jax
import jax.numpy as jnp
import numpy as np
from jax import lax
from jax.experimental import pallas as pl
from jax.experimental.pallas import tpu as pltpu
from jax.sharding import PartitionSpec as P

DIMS = (4, 4, 2, 2)
SLOTS = 2
VMEM_LIMIT = 4 * 2**20

HOME = (0, 0, 0)
ROUNDS = (
    (
        ("M1", (HOME,)),
        ("M2", (HOME,)),
        ("X", (HOME,)),
        ("P2", (HOME,)),
        ("P1", (HOME,)),
    ),
    (
        ("P1", ((0, 0, 1), (0, 3, 0))),
        ("M2", ((0, 1, 0), (0, 0, 1))),
        ("X", ((0, 0, 3), (0, 1, 0))),
        ("M1", ((1, 0, 0), (0, 0, 3))),
        ("P2", ((0, 3, 0), (1, 0, 0))),
    ),
    (
        ("M2", ((1, 3, 0), (1, 0, 1))),
        ("P2", ((0, 3, 3), (0, 1, 3))),
        ("X", ((0, 0, 2), (0, 1, 1))),
        ("M1", ((0, 1, 1), (1, 0, 3))),
        ("P1", ((0, 3, 3), (1, 0, 3))),
    ),
    (
        ("M2", ((1, 2, 0), (1, 3, 1))),
        ("P2", ((1, 2, 0),)),
        ("D1", ((1, 0, 2),)),
        ("X", ((0, 2, 1),)),
        ("M1", ((0, 1, 2),)),
    ),
)
LATE = ((), (), ("P1", "M2"), ("P2",))
WIDTH = (2, 4)
STEPS = {"P1": (0, 1), "M1": (0, -1), "D1": (0, 2), "D2": (1, 2), "P2": (1, 1), "M2": (1, -1)}


def row_of(place):
    return int(np.ravel_multi_index(place, DIMS))


def pairs_of(channel):
    pairs = []
    for place in np.ndindex(*DIMS):
        to = list(place)
        if channel == "X":
            to[2] = 1 - to[2]
        elif channel == "C":
            to[3] = 1 - to[3]
        else:
            axis, by = STEPS[channel]
            axis = (axis + place[2]) % 2
            to[axis] = (to[axis] + by * (1 - 2 * place[3])) % DIMS[axis]
        pairs.append((row_of(place), row_of(to)))
    return pairs


def arrived(channel, unit):
    t, a, b = unit
    if channel == "X":
        return (1 - t, b, a)
    axis, by = STEPS[channel]
    return (t, (a - by) % 4, b) if axis == 0 else (t, a, (b - by) % 4)


def send(x, channel):
    return lax.ppermute(x, "row", pairs_of(channel))


def owner_of(where, unit, core_flip):
    t, a, b = unit
    row = where[0]
    h = (row >> 1) & 1
    sign = 1 - 2 * ((row & 1) ^ core_flip)
    a, b = a * sign, b * sign
    z = ((row >> 4) + a + h * (b - a)) & 3
    y = (((row >> 2) & 3) + b + h * (a - b)) & 3
    return (((z * 4 + y) * 2 + (h ^ t)) << 1) + ((row & 1) ^ core_flip)


def pack_kernel(layout, begin, block, where, codes, *refs):
    arrays, out = refs[: len(layout)], refs[-1]
    n = begin
    for array, units in zip(arrays, layout):
        size = array.shape[0] // len(units)
        for at, unit in enumerate(units):
            owner = owner_of(where, unit, 0)
            for k in range(SLOTS):

                @pl.when(k < codes[SLOTS, owner])
                def _():
                    start = pl.multiple_of(at * size + (codes[k, owner] & 3) * block, block)
                    out[n * SLOTS + k] = array[pl.ds(start, block), :]

            n += 1


def pack(group, where, codes, block, total, into=None):
    arrays, layout = [x for x, _ in group], tuple(us for _, us in group)
    channels = arrays[0].shape[1]
    count = sum(map(len, layout))
    vmem = pl.BlockSpec(memory_space=pltpu.VMEM)
    operands = [where, codes, *arrays] + ([] if into is None else [into])
    return pl.pallas_call(
        functools.partial(pack_kernel, layout, 0 if into is None else total - count, block),
        out_shape=jax.ShapeDtypeStruct((total * SLOTS, block, channels), jnp.bfloat16),
        in_specs=[pl.BlockSpec(memory_space=pltpu.SMEM)] * 2 + [vmem] * (len(operands) - 2),
        out_specs=vmem,
        input_output_aliases={} if into is None else {len(operands) - 1: 0},
        cost_estimate=pl.CostEstimate(
            flops=0, bytes_accessed=count * SLOTS * block * channels * 4, transcendentals=0
        ),
        compiler_params=pltpu.CompilerParams(vmem_limit_bytes=VMEM_LIMIT),
        name="pack",
    )(*operands)


def terms_kernel(layout, half, where, codes, blocks, *refs):
    arrays, refs = refs[: len(layout)], refs[len(layout) :]
    total_in = None
    if len(refs) > 2:
        total_in, refs = refs[0], refs[1:]
    total, owners = refs
    block = blocks.shape[-1]
    base = where[1] * 4
    size = total.shape[0]

    for n, (unit, flip) in enumerate([(u, flip) for us, flip in layout for u in us]):
        owners[n] = owner_of(where, unit, flip)
    if total_in is None:
        total[...] = jnp.zeros_like(total)
    elif total_in.shape == total.shape:
        total[...] = total_in[...]
    else:
        total[...] = total_in[half * size : (half + 1) * size, :]

    def target_of(owner, k):
        return ((codes[k, owner] >> 2) + base) & 7

    def counts(owner, k):
        live = k < codes[SLOTS, owner]
        return live if half is None else live & (target_of(owner, k) >> 2 == half)

    def sweep(begin, count, features, width):
        def products(tasks):
            found = []
            for i, k in tasks:
                owner = owners[begin + i]
                target = target_of(owner, k)
                if half is not None:
                    target = target & 3
                rows = pl.ds(pl.multiple_of(target * block, block), block)
                product = jnp.dot(
                    blocks[owner, k], features(i, codes[k, owner], k), preferred_element_type=jnp.float32
                )
                found.append((rows, product))
            for rows, product in found:
                total[rows, :] += product

        def some(first, units):
            tasks = [(first + i, k) for i in range(units) for k in range(SLOTS)]
            whole = functools.reduce(jnp.logical_and, [counts(owners[begin + i], k) for i, k in tasks])

            @pl.when(whole)
            def _():
                products(tasks)

            @pl.when(jnp.logical_not(whole))
            def _():
                def one(task, carry):
                    i, k = first + task // SLOTS, task % SLOTS

                    @pl.when(counts(owners[begin + i], k))
                    def _():
                        products([(i, k)])

                    return carry

                lax.fori_loop(0, len(tasks), one, 0)

        width = min(count, width if half is None else 1)
        steps = count // width
        if steps == 1:
            some(0, width)
        elif steps:

            def step(n, carry):
                some(n * width, width)
                return carry

            lax.fori_loop(0, steps, step, 0)
        if count % width:
            some(steps * width, count % width)

    begin = 0
    for array, (us, flip) in zip(arrays, layout):
        unit_rows = array.shape[0] // len(us)

        def features(i, code, k, array=array, unit_rows=unit_rows, flip=flip):
            if flip:
                return array[i * SLOTS + k]
            return array[pl.ds(pl.multiple_of(i * unit_rows + (code & 3) * block, block), block), :]

        sweep(begin, len(us), features, WIDTH[flip])
        begin += len(us)


def terms(group, packed, running, where, codes, blocks, half=None):
    sources = [(x, us, 0) for x, us in group] + [(x, us, 1) for x, us in packed]
    layout = tuple((us, flip) for _, us, flip in sources)
    block = blocks.shape[-1]
    channels = sources[0][0].shape[-1]
    n = sum(len(us) for us, _ in layout) * SLOTS
    vmem = pl.BlockSpec(memory_space=pltpu.VMEM)
    operands = [where, codes, blocks] + [x for x, _, _ in sources] + ([] if running is None else [running])
    return pl.pallas_call(
        functools.partial(terms_kernel, layout, half),
        out_shape=jax.ShapeDtypeStruct((8 * block if half is None else 4 * block, channels), jnp.float32),
        in_specs=[pl.BlockSpec(memory_space=pltpu.SMEM)] * 2 + [vmem] * (len(operands) - 2),
        out_specs=vmem,
        scratch_shapes=[pltpu.SMEM((n // SLOTS,), jnp.int32)],
        compiler_params=pltpu.CompilerParams(vmem_limit_bytes=VMEM_LIMIT),
        cost_estimate=pl.CostEstimate(
            flops=2 * n * block * block * channels,
            bytes_accessed=n * (block * block + block * channels) * 2,
            transcendentals=0,
        ),
        name="terms",
    )(*operands)


def load_kernel(source, out, sem):
    copy = pltpu.make_async_copy(source, out, sem)
    copy.start()
    copy.wait()


def load(blocks):
    return pl.pallas_call(
        load_kernel,
        out_shape=pltpu.VMEM(blocks.shape, blocks.dtype),
        in_specs=[pl.BlockSpec(memory_space=pltpu.HBM)],
        out_specs=pl.BlockSpec(memory_space=pltpu.VMEM),
        scratch_shapes=[pltpu.SemaphoreType.DMA(())],
        compiler_params=pltpu.CompilerParams(vmem_limit_bytes=VMEM_LIMIT),
        cost_estimate=pl.CostEstimate(flops=0, bytes_accessed=2 * blocks.size, transcendentals=0),
        name="load",
    )(pltpu.with_memory_space_constraint(blocks, pltpu.HBM))


def after(xs, *others):
    return list(lax.optimization_barrier((tuple(xs), others))[0])


def body(features, blocks, codes, counts, weight, bias):
    block = blocks.shape[-1]
    size = features.shape[0]
    where = jnp.stack([lax.axis_index("row"), lax.axis_index("rep")]).astype(jnp.int32)
    blocks = blocks.reshape(blocks.shape[2:])
    codes = jnp.concatenate([codes.reshape(codes.shape[2:]).T, counts.reshape(1, -1)])
    other_codes = send(codes, "C")
    held = {HOME: (features, 0)}
    arrays = [(features, (HOME,))]

    def payload(units):
        for x, us in arrays:
            if set(us) == set(units):
                return x, us
        x = [held[u][0][held[u][1] * size : (held[u][1] + 1) * size] for u in units]
        return x[0] if len(x) == 1 else jnp.concatenate(x), units

    def exchange(number, payloads, late, first, second):
        group = []
        payloads = [p for p in payloads if p[0] not in late] + [p for p in payloads if p[0] in late]
        for channel, x, units in payloads:
            x = after([x], *first, *(second if channel in late else ()))[0] if first else x
            x, units = send(x, channel), tuple(arrived(channel, u) for u in units)
            for at, u in enumerate(units):
                assert u not in held, u
                held[u] = (x, at)
            group.append((x, units))
        arrays.extend(group)
        return group

    def names(group):
        return tuple(u for _, us in group for u in us)

    def hold(group, *others):
        return [(x, us) for x, (_, us) in zip(after([x for x, _ in group], *others), group)]

    def payloads(number):
        return [(c,) + payload(us) for c, us in ROUNDS[number]]

    def xs(group):
        return [x for x, _ in group]

    def add(group, packed, running, half=None):
        return terms(group, packed, running, where, codes, blocks, half)

    group = exchange(0, payloads(0), (), (), ())

    moves = payloads(1)
    early, have = [], set()
    for x, us in [(features, (HOME,))] + [(x, us) for _, x, us in moves] + group:
        if not have & set(us):
            early.append((x, us))
            have |= set(us)
    group = exchange(1, moves, (), [*xs(group), other_codes], ())
    blocks = load(blocks)
    count = len(names(early)) + len(names(group))
    packed = pack(early, where, other_codes, block, count)

    moves = payloads(2)
    group = hold(group, packed, blocks)
    packed = pack(group, where, other_codes, block, count, packed)
    first = xs(group) + [packed]
    ready = early + group
    packed = [(send(packed, "C"), names(ready))]
    group = exchange(2, moves, LATE[2], first, xs(packed))
    running = add(ready, packed, None)

    moves = payloads(3)
    group = hold(group, running)
    packed = pack(group, where, other_codes, block, len(names(group)))
    first = xs(group) + [packed]
    ready = group
    packed = [(send(packed, "C"), names(group))]
    group = exchange(3, moves, LATE[3], first, xs(packed))
    running = add(ready, packed, running)

    group = hold(group, running)
    packed = pack(group, where, other_codes, block, len(names(group)))
    packed = [(send(packed, "C"), names(group))]
    sent = add(group, [], running, 1)
    sent = add([], packed, sent, 1)
    kept = add(group, packed, running, 0)
    received = lax.ppermute(sent.astype(jnp.bfloat16), "rep", [(0, 1), (1, 0)])
    shares = (kept + received.astype(jnp.float32)).astype(jnp.bfloat16)
    hidden = jnp.dot(shares, weight, preferred_element_type=jnp.float32) + bias
    return jnp.maximum(hidden, 0.0).astype(jnp.bfloat16)


def solution(mesh):
    placed = (
        P(("row", "rep"), None),
        P("row", "rep", None, None, None, None),
        P("row", "rep", None, None),
        P("row", "rep", None),
        P(),
        P(),
    )
    return jax.shard_map(
        body, mesh=mesh, in_specs=placed, out_specs=P(("row", "rep"), None), check_vma=False
    )
```

```python
import functools

import jax
import jax.numpy as jnp
import numpy as np
from jax import lax
from jax.experimental import pallas as pl
from jax.experimental.pallas import tpu as pltpu
from jax.sharding import PartitionSpec as P

DIMS = (4, 4, 2, 2)
SLOTS = 2
VMEM_LIMIT = 4 * 2**20

HOME = (0, 0, 0)
ROUNDS = (
    (
        ("M1", (HOME,)),
        ("M2", (HOME,)),
        ("X", (HOME,)),
        ("P2", (HOME,)),
        ("P1", (HOME,)),
    ),
    (
        ("P1", ((0, 0, 1), (0, 3, 0))),
        ("M2", ((0, 1, 0), (0, 0, 1))),
        ("X", ((0, 0, 3), (0, 1, 0))),
        ("M1", ((1, 0, 0), (0, 0, 3))),
        ("P2", ((0, 3, 0), (1, 0, 0))),
    ),
    (
        ("M2", ((1, 3, 0), (1, 0, 1))),
        ("P2", ((0, 3, 3), (0, 1, 3))),
        ("X", ((0, 0, 2), (0, 1, 1))),
        ("M1", ((0, 1, 1), (1, 0, 3))),
        ("P1", ((0, 3, 3), (1, 0, 3))),
    ),
    (
        ("M2", ((1, 2, 0), (1, 3, 1))),
        ("P2", ((1, 2, 0),)),
        ("D1", ((1, 0, 2),)),
        ("X", ((0, 2, 1),)),
        ("M1", ((0, 1, 2),)),
    ),
)
LATE = ((), (), ("P1", "M2"), ("P2",))
WIDTH = (2, 4)
STEPS = {"P1": (0, 1), "M1": (0, -1), "D1": (0, 2), "D2": (1, 2), "P2": (1, 1), "M2": (1, -1)}


def row_of(place):
    return int(np.ravel_multi_index(place, DIMS))


def pairs_of(channel):
    pairs = []
    for place in np.ndindex(*DIMS):
        to = list(place)
        if channel == "X":
            to[2] = 1 - to[2]
        elif channel == "C":
            to[3] = 1 - to[3]
        else:
            axis, by = STEPS[channel]
            axis = (axis + place[2]) % 2
            to[axis] = (to[axis] + by * (1 - 2 * place[3])) % DIMS[axis]
        pairs.append((row_of(place), row_of(to)))
    return pairs


def arrived(channel, unit):
    t, a, b = unit
    if channel == "X":
        return (1 - t, b, a)
    axis, by = STEPS[channel]
    return (t, (a - by) % 4, b) if axis == 0 else (t, a, (b - by) % 4)


def send(x, channel):
    return lax.ppermute(x, "row", pairs_of(channel))


def owner_of(where, unit, core_flip):
    t, a, b = unit
    row = where[0]
    h = (row >> 1) & 1
    sign = 1 - 2 * ((row & 1) ^ core_flip)
    a, b = a * sign, b * sign
    z = ((row >> 4) + a + h * (b - a)) & 3
    y = (((row >> 2) & 3) + b + h * (a - b)) & 3
    return (((z * 4 + y) * 2 + (h ^ t)) << 1) + ((row & 1) ^ core_flip)


def pack_kernel(layout, begin, block, where, codes, *refs):
    arrays, out = refs[: len(layout)], refs[-1]
    n = begin
    for array, units in zip(arrays, layout):
        size = array.shape[0] // len(units)
        for at, unit in enumerate(units):
            owner = owner_of(where, unit, 0)
            for k in range(SLOTS):

                @pl.when(k < codes[SLOTS, owner])
                def _():
                    start = pl.multiple_of(at * size + (codes[k, owner] & 3) * block, block)
                    out[n * SLOTS + k] = array[pl.ds(start, block), :]

            n += 1


def pack(group, where, codes, block, total, into=None):
    arrays, layout = [x for x, _ in group], tuple(us for _, us in group)
    channels = arrays[0].shape[1]
    count = sum(map(len, layout))
    vmem = pl.BlockSpec(memory_space=pltpu.VMEM)
    operands = [where, codes, *arrays] + ([] if into is None else [into])
    return pl.pallas_call(
        functools.partial(pack_kernel, layout, 0 if into is None else total - count, block),
        out_shape=jax.ShapeDtypeStruct((total * SLOTS, block, channels), jnp.bfloat16),
        in_specs=[pl.BlockSpec(memory_space=pltpu.SMEM)] * 2 + [vmem] * (len(operands) - 2),
        out_specs=vmem,
        input_output_aliases={} if into is None else {len(operands) - 1: 0},
        cost_estimate=pl.CostEstimate(
            flops=0, bytes_accessed=count * SLOTS * block * channels * 4, transcendentals=0
        ),
        compiler_params=pltpu.CompilerParams(vmem_limit_bytes=VMEM_LIMIT),
        name="pack",
    )(*operands)


def terms_kernel(layout, half, where, codes, blocks, *refs):
    arrays, refs = refs[: len(layout)], refs[len(layout) :]
    total_in = None
    if len(refs) > 2:
        total_in, refs = refs[0], refs[1:]
    total, owners = refs
    block = blocks.shape[-1]
    base = where[1] * 4
    size = total.shape[0]

    for n, (unit, flip) in enumerate([(u, flip) for us, flip in layout for u in us]):
        owners[n] = owner_of(where, unit, flip)
    if total_in is None:
        total[...] = jnp.zeros_like(total)
    elif total_in.shape != total.shape:
        total[...] = total_in[half * size : (half + 1) * size, :]

    def target_of(owner, k):
        return ((codes[k, owner] >> 2) + base) & 7

    def counts(owner, k):
        live = k < codes[SLOTS, owner]
        return live if half is None else live & (target_of(owner, k) >> 2 == half)

    def sweep(begin, count, features, width):
        def products(tasks):
            found = []
            for i, k in tasks:
                owner = owners[begin + i]
                target = target_of(owner, k)
                if half is not None:
                    target = target & 3
                rows = pl.ds(pl.multiple_of(target * block, block), block)
                product = jnp.dot(
                    blocks[owner, k], features(i, codes[k, owner], k), preferred_element_type=jnp.float32
                )
                found.append((rows, product))
            for rows, product in found:
                total[rows, :] += product

        def some(first, units):
            tasks = [(first + i, k) for i in range(units) for k in range(SLOTS)]
            whole = functools.reduce(jnp.logical_and, [counts(owners[begin + i], k) for i, k in tasks])

            @pl.when(whole)
            def _():
                products(tasks)

            @pl.when(jnp.logical_not(whole))
            def _():
                def one(task, carry):
                    i, k = first + task // SLOTS, task % SLOTS

                    @pl.when(counts(owners[begin + i], k))
                    def _():
                        products([(i, k)])

                    return carry

                lax.fori_loop(0, len(tasks), one, 0)

        width = min(count, width if half is None else 1)
        steps = count // width
        if steps == 1:
            some(0, width)
        elif steps:

            def step(n, carry):
                some(n * width, width)
                return carry

            lax.fori_loop(0, steps, step, 0)
        if count % width:
            some(steps * width, count % width)

    begin = 0
    for array, (us, flip) in zip(arrays, layout):
        unit_rows = array.shape[0] // len(us)

        def features(i, code, k, array=array, unit_rows=unit_rows, flip=flip):
            if flip:
                return array[i * SLOTS + k]
            return array[pl.ds(pl.multiple_of(i * unit_rows + (code & 3) * block, block), block), :]

        sweep(begin, len(us), features, WIDTH[flip])
        begin += len(us)


def terms(group, packed, running, where, codes, blocks, half=None):
    sources = [(x, us, 0) for x, us in group] + [(x, us, 1) for x, us in packed]
    layout = tuple((us, flip) for _, us, flip in sources)
    block = blocks.shape[-1]
    channels = sources[0][0].shape[-1]
    n = sum(len(us) for us, _ in layout) * SLOTS
    vmem = pl.BlockSpec(memory_space=pltpu.VMEM)
    operands = [where, codes, blocks] + [x for x, _, _ in sources] + ([] if running is None else [running])
    shape = (8 * block if half is None else 4 * block, channels)
    same = running is not None and running.shape == shape
    return pl.pallas_call(
        functools.partial(terms_kernel, layout, half),
        out_shape=jax.ShapeDtypeStruct(shape, jnp.float32),
        in_specs=[pl.BlockSpec(memory_space=pltpu.SMEM)] * 2 + [vmem] * (len(operands) - 2),
        out_specs=vmem,
        input_output_aliases={len(operands) - 1: 0} if same else {},
        scratch_shapes=[pltpu.SMEM((n // SLOTS,), jnp.int32)],
        compiler_params=pltpu.CompilerParams(vmem_limit_bytes=VMEM_LIMIT),
        cost_estimate=pl.CostEstimate(
            flops=2 * n * block * block * channels,
            bytes_accessed=n * (block * block + block * channels) * 2,
            transcendentals=0,
        ),
        name="terms",
    )(*operands)


def load_kernel(source, out, sem):
    copy = pltpu.make_async_copy(source, out, sem)
    copy.start()
    copy.wait()


def load(blocks):
    return pl.pallas_call(
        load_kernel,
        out_shape=pltpu.VMEM(blocks.shape, blocks.dtype),
        in_specs=[pl.BlockSpec(memory_space=pltpu.HBM)],
        out_specs=pl.BlockSpec(memory_space=pltpu.VMEM),
        scratch_shapes=[pltpu.SemaphoreType.DMA(())],
        compiler_params=pltpu.CompilerParams(vmem_limit_bytes=VMEM_LIMIT),
        cost_estimate=pl.CostEstimate(flops=0, bytes_accessed=2 * blocks.size, transcendentals=0),
        name="load",
    )(pltpu.with_memory_space_constraint(blocks, pltpu.HBM))


def after(xs, *others):
    return list(lax.optimization_barrier((tuple(xs), others))[0])


def body(features, blocks, codes, counts, weight, bias):
    block = blocks.shape[-1]
    size = features.shape[0]
    where = jnp.stack([lax.axis_index("row"), lax.axis_index("rep")]).astype(jnp.int32)
    blocks = blocks.reshape(blocks.shape[2:])
    codes = jnp.concatenate([codes.reshape(codes.shape[2:]).T, counts.reshape(1, -1)])
    other_codes = send(codes, "C")
    held = {HOME: (features, 0)}
    arrays = [(features, (HOME,))]

    def payload(units):
        for x, us in arrays:
            if set(us) == set(units):
                return x, us
        x = [held[u][0][held[u][1] * size : (held[u][1] + 1) * size] for u in units]
        return x[0] if len(x) == 1 else jnp.concatenate(x), units

    def exchange(number, payloads, late, first, second):
        group = []
        payloads = [p for p in payloads if p[0] not in late] + [p for p in payloads if p[0] in late]
        for channel, x, units in payloads:
            x = after([x], *first, *(second if channel in late else ()))[0] if first else x
            x, units = send(x, channel), tuple(arrived(channel, u) for u in units)
            for at, u in enumerate(units):
                assert u not in held, u
                held[u] = (x, at)
            group.append((x, units))
        arrays.extend(group)
        return group

    def names(group):
        return tuple(u for _, us in group for u in us)

    def hold(group, *others):
        return [(x, us) for x, (_, us) in zip(after([x for x, _ in group], *others), group)]

    def payloads(number):
        return [(c,) + payload(us) for c, us in ROUNDS[number]]

    def xs(group):
        return [x for x, _ in group]

    def add(group, packed, running, half=None):
        return terms(group, packed, running, where, codes, blocks, half)

    group = exchange(0, payloads(0), (), (), ())

    moves = payloads(1)
    early, have = [], set()
    for x, us in [(features, (HOME,))] + [(x, us) for _, x, us in moves] + group:
        if not have & set(us):
            early.append((x, us))
            have |= set(us)
    group = exchange(1, moves, (), [*xs(group), other_codes], ())
    blocks = load(blocks)
    count = len(names(early)) + len(names(group))
    packed = pack(early, where, other_codes, block, count)

    moves = payloads(2)
    group = hold(group, packed, blocks)
    packed = pack(group, where, other_codes, block, count, packed)
    first = xs(group) + [packed]
    ready = early + group
    packed = [(send(packed, "C"), names(ready))]
    group = exchange(2, moves, LATE[2], first, xs(packed))
    running = add(ready, packed, None)

    moves = payloads(3)
    group = hold(group, running)
    packed = pack(group, where, other_codes, block, len(names(group)))
    first = xs(group) + [packed]
    ready = group
    packed = [(send(packed, "C"), names(group))]
    group = exchange(3, moves, LATE[3], first, xs(packed))
    running = add(ready, packed, running)

    group = hold(group, running)
    packed = pack(group, where, other_codes, block, len(names(group)))
    packed = [(send(packed, "C"), names(group))]
    sent = add(group, [], running, 1)
    sent = add([], packed, sent, 1)
    kept = add(group, packed, running, 0)
    received = lax.ppermute(sent.astype(jnp.bfloat16), "rep", [(0, 1), (1, 0)])
    shares = (kept + received.astype(jnp.float32)).astype(jnp.bfloat16)
    hidden = jnp.dot(shares, weight, preferred_element_type=jnp.float32) + bias
    return jnp.maximum(hidden, 0.0).astype(jnp.bfloat16)


def solution(mesh):
    placed = (
        P(("row", "rep"), None),
        P("row", "rep", None, None, None, None),
        P("row", "rep", None, None),
        P("row", "rep", None),
        P(),
        P(),
    )
    return jax.shard_map(
        body, mesh=mesh, in_specs=placed, out_specs=P(("row", "rep"), None), check_vma=False
    )
```
